1024 devices in a mesh: fsdp: 64 (over z, x_hi), tp: 8 (over y, x_lo), rep: 2 (over core).
Axes of the slice: x: 4 (x_hi: 2, x_lo: 2; x = x_hi * 2 + x_lo), y: 4, z: 32, core: 2. Of those that a mesh axis runs over, the one named last changes fastest.
Arguments:
- base_weight: bfloat16 [64, 1024, 7168], P('fsdp', 'tp'), may hold values from -0.125 to 0.125
- delta_codes: bfloat16 [64, 1024, 7168], P(None, ('tp', 'rep'), 'fsdp'), may hold values from -448 to 448
- block_scales: float32 [64, 8, 56], P('fsdp', 'tp'), may hold values from 2e-05 to 0.0001
- hidden_acts: bfloat16 [2, 512, 8, 2, 1024], P(None, ('fsdp', 'rep'), None, None, 'tp'), may hold values from -6 to 6
- expert_ids: int32 [2, 512, 8], P(None, ('fsdp', 'rep')), may hold values from 0 to 31, all different within a row; in each aligned block of 4 rows (0 to 3, 4 to 7, ..., all dimensions but the last counted through in order) at most 2 rows name the same one
- gate_weights: float32 [2, 512, 8], P(None, ('fsdp', 'rep')), may hold values from 0.1 to 1
Outputs:
- mixed_rows: bfloat16 [2, 512, 7168], P(None, ('fsdp', 'rep'), 'tp')
The draws below stay inside these ranges and needn't reach their ends.
Inputs may be any that keep to these rules, and one draw needn't show every extreme that they name: `expert_ids`: within the 4 rows of one device in one step (aligned blocks), no expert is named by more than 2 rows, a bound that some block reaches; a row names 8 different experts.
All inputs are finite; a program needn't handle non-finite values.
Results may differ from the reference program's by a relative error of at most 0.015.
Values may be sent and summed in bfloat16 or wider, within the bound.
A program may use at most 64 MiB of HBM per device.

```python
import math
import jax
import jax.numpy as jnp
import numpy as np
from jax import lax

D = 7168
H = 2048
TOP = 8
BLOCK = 128
STEPS = 2
ROWS_DEV = 4
EXPERTS = 32
CAP = 2
ROWS = 512
N_TP = 8


def level_of(stream_key, dims, cuts, low, high):
    def one(axis_at, shards_of):
        steps = jax.random.uniform(jax.random.fold_in(jax.random.fold_in(stream_key, 6), axis_at), (shards_of,), jnp.float32, low / len(cuts), high / len(cuts))
        return jnp.repeat(jnp.exp(steps), dims[axis_at] // shards_of).reshape((-1,) + (1,) * (len(dims) - axis_at - 1))

    level = one(*cuts[0])
    for cut in cuts[1:]:
        level = level * one(*cut)
    return level


def assign_block(stream_key, own, number, rows, count, top, bound, lean):
    sequence = jax.random.permutation(stream_key, count)
    packed, common = shares(count, rows * top, bound, lean, True), shares(count, rows * top, bound, lean, False)
    places = jnp.arange(count)

    def named(tallies, offset_by):
        used = int((tallies > 0).sum())
        fixed = max(1, used // 4)
        passed = fixed + (places - fixed + offset_by * (used - fixed)) % max(1, count - fixed)
        return jnp.zeros((count,), jnp.int32).at[sequence[jnp.where(places < fixed, places, passed)]].set(jnp.asarray(tallies, jnp.int32))

    tallies = jnp.where(number % 4 == 0, named(packed, number // 4), named(common, number - number // 4 - 1))
    mixed = jax.random.permutation(jax.random.fold_in(own, 3), count)
    source_of, receiver = mixed[0:count // 2 * 2:2], mixed[1:count // 2 * 2:2]
    slack = jnp.minimum(tallies[source_of] - 1, bound - tallies[receiver]) // 2
    slack = jnp.where((source_of == sequence[0]) | (receiver == sequence[0]) | (tallies[receiver] == 0), 0, jnp.maximum(slack, 0))
    passed = jax.random.randint(jax.random.fold_in(own, 4), (count // 2,), 0, 1 << 20) % (slack + 1)
    tallies = tallies.at[source_of].add(-passed).at[receiver].add(passed)
    items = jnp.searchsorted(jnp.cumsum(tallies), jnp.arange(rows * top), side="right").astype(jnp.int32)
    listing = items.reshape(top, rows).T
    listing = listing[jax.random.permutation(jax.random.fold_in(own, 1), rows)]
    offset_by = jax.random.randint(jax.random.fold_in(own, 2), (rows, 1), 0, top)
    return jnp.take_along_axis(listing, (jnp.arange(top)[None, :] + offset_by) % top, axis=1)


def shares(amount, total, bound, lean, full):
    weights = [(1 << 20) // math.isqrt(grade ** lean) + 1 for grade in range(1, amount + 1)]
    largest = bound if full else min(bound, max(-(-total // amount), total * weights[0] // sum(weights)))
    least = 1 if total - largest >= amount - 1 else 0
    holding, spare = [largest] + [least] * (amount - 1), total - largest - least * (amount - 1)
    while spare > 0:
        candidates = [i for i in range(1, amount) if holding[i] < largest] or [i for i in range(1, amount) if holding[i] < bound]
        whole, budget = sum([weights[i] for i in candidates]), spare
        for i in candidates:
            extra = min(bound - holding[i], max(1, budget * weights[i] // whole), spare)
            holding[i] = holding[i] + extra
            spare = spare - extra
    return np.array(holding)


def bell_draw(rng, shape, width, bound, cuts=(), kind=jnp.bfloat16):
    entries = width * jax.random.normal(rng, shape, jnp.float32)
    if cuts:
        entries = entries * level_of(rng, shape, cuts, -0.22, 0.18)
    return jnp.clip(entries, -bound, bound).astype(kind)


def setup_inputs(seed: int = 0) -> dict:
    streams_of = jax.random.split(jax.random.key(seed), 7)
    base_weight = bell_draw(streams_of[0], (2 * EXPERTS, H // 2, D), H ** -0.5, 0.125, ((0, 64), (1, 8)))
    delta_codes = jnp.clip(jax.random.uniform(streams_of[1], (2 * EXPERTS, H // 2, D), jnp.float32, -448.0, 448.0) * level_of(streams_of[1], (2 * EXPERTS, H // 2, D), ((1, 16), (2, 64)), -0.4, 0.0), -448.0, 448.0).astype(jnp.bfloat16)
    block_scales = jnp.clip(jnp.exp(math.log(0.0001) - 1.609438 * jax.random.uniform(streams_of[2], (2 * EXPERTS, H // 2 // BLOCK, D // BLOCK), jnp.float32) ** level_of(streams_of[2], (2 * EXPERTS, H // 2 // BLOCK, D // BLOCK), ((0, 64), (1, 8)), -0.2, 0.2)), 1.9999999494757503e-05, 0.0001)
    hidden_acts = bell_draw(streams_of[3], (STEPS, ROWS, TOP, 2, H // 2), 1.0, 6.0, ((1, 128), (4, 8)))
    expert_ids_keys = jax.random.split(jax.random.fold_in(streams_of[4], 1), STEPS * ROWS // ROWS_DEV)
    expert_ids_turns = jax.random.permutation(jax.random.fold_in(streams_of[4], 3), STEPS * ROWS // ROWS_DEV)
    expert_ids = jax.vmap(lambda own, number: assign_block(jax.random.fold_in(streams_of[4], 2), own, number, ROWS_DEV, EXPERTS, TOP, CAP, 2))(expert_ids_keys, expert_ids_turns).reshape((STEPS, ROWS, TOP))
    gate_weights = jnp.clip(0.1 + 0.9 * jax.random.uniform(streams_of[5], (STEPS, ROWS, TOP), jnp.float32) ** level_of(streams_of[5], (STEPS, ROWS, TOP), ((1, 128),), -0.2, 0.2), 0.1, 1.0)
    return dict(base_weight=base_weight, delta_codes=delta_codes, block_scales=block_scales, hidden_acts=hidden_acts, expert_ids=expert_ids, gate_weights=gate_weights)


def reference(base_weight, delta_codes, block_scales, hidden_acts, expert_ids, gate_weights):
    half_units = base_weight.shape[1]
    model_width = base_weight.shape[2]
    group_units = half_units // N_TP
    slot_count = STEPS * ROWS * TOP
    slot_limit = CAP * STEPS * ROWS // ROWS_DEV
    flat_ids = expert_ids.reshape(slot_count)
    flat_gates = gate_weights.reshape(slot_count)
    flat_acts = hidden_acts.reshape(slot_count, 2, N_TP, group_units)
    row_of_slot = jnp.arange(slot_count, dtype=jnp.int32) // TOP
    slot_range = jnp.arange(slot_limit, dtype=jnp.int32)

    def one_expert(running, expert):
        chosen = flat_ids == expert
        picked = jnp.nonzero(chosen, size=slot_limit, fill_value=0)[0].astype(jnp.int32)
        filled = jnp.sum(chosen.astype(jnp.int32))
        first_row = (2 * expert).astype(jnp.int32)
        scale_pair = lax.dynamic_slice_in_dim(block_scales, first_row, 2, 0)
        scale_full = jnp.repeat(jnp.repeat(scale_pair, BLOCK, axis=1), BLOCK, axis=2)
        base_pair = lax.dynamic_slice_in_dim(base_weight, first_row, 2, 0).astype(jnp.float32)
        code_pair = lax.dynamic_slice_in_dim(delta_codes, first_row, 2, 0).astype(jnp.float32)
        pair_weights = (base_pair + code_pair * scale_full).astype(jnp.bfloat16)
        pair_weights = pair_weights.reshape(2, N_TP, group_units, model_width).astype(jnp.float32)
        gathered = flat_acts[picked].astype(jnp.float32)
        partial_value = jnp.einsum("mpgh,pghd->mpgd", gathered, pair_weights).astype(jnp.bfloat16)
        summed = jnp.sum(partial_value.astype(jnp.float32), axis=(1, 2))
        factor = jnp.where(slot_range < filled, flat_gates[picked], jnp.zeros((), jnp.float32))
        return running.at[row_of_slot[picked]].add(summed * factor[:, None]), None

    start_sum = jnp.zeros((STEPS * ROWS, D), jnp.float32)
    result, _ = lax.scan(one_expert, start_sum, jnp.arange(EXPERTS, dtype=jnp.int32))
    return result.reshape(STEPS, ROWS, D).astype(jnp.bfloat16)
```

```python
import jax
import jax.numpy as jnp
from jax import lax
from jax.experimental import pallas as pl
from jax.experimental.pallas import tpu as pltpu
from jax.sharding import PartitionSpec as P

MESH = pl.DeviceIdType.MESH
BF16 = jnp.bfloat16
F32 = jnp.float32


def position():
    f, t, r = lax.axis_index("fsdp"), lax.axis_index("tp"), lax.axis_index("rep")
    return f // 2, f % 2, t, r


def push(src, dst, send_sem, recv_sem, z, xh, t, r):
    return pltpu.make_async_remote_copy(
        src_ref=src,
        dst_ref=dst,
        send_sem=send_sem,
        recv_sem=recv_sem,
        device_id=(z * 2 + xh, t, r),
        device_id_type=MESH,
    )


def loop(low, high, body):
    def step(i, carry):
        body(i)
        return carry

    lax.fori_loop(low, high, step, jnp.int32(0))


def spread_kernel(
    planes, groups, disp, quarters, base, codes,
    slots, ring, weights, swapped,
    quad, local_sem, quad_send, quad_recv, disp_send, disp_recv, tp_send, tp_recv,
    w_send, w_recv, pair_send, pair_recv, code_send, code_recv,
    right_send, right_recv, left_send, left_recv,
):
    z, xh, t, r = position()
    home = xh * 2 + r
    place = xh * groups + t
    half_units = base.shape[0] // 2
    width = weights.shape[2]

    def hello(to_z, to_xh, to_t, to_r):
        pl.semaphore_signal(
            pltpu.get_barrier_semaphore(),
            inc=1,
            device_id=(to_z * 2 + to_xh, to_t, to_r),
            device_id_type=MESH,
        )

    loop(1, planes, lambda d: hello((z + d) % planes, xh, t, r))
    def hello_plane(j):
        other = (place + j) % (2 * groups)
        hello(z, other // groups, other % groups, r)
    loop(1, 2 * groups, hello_plane)
    hello(z, xh, t, 1 - r)
    hello(z, 1 - xh, t, 1 - r)

    def quad_copy(i):
        to = (home + i) % 4
        return push(quarters.at[to], quad.at[home], quad_send.at[i], quad_recv.at[i], z, to // 2, t, to % 2)

    def disp_copy(d):
        to = (z + d) % planes
        return push(disp.at[to], slots.at[t, z], disp_send.at[d], disp_recv.at[d], to, xh, t, r)

    def tp_copy(j):
        return push(slots.at[t], slots.at[t], tp_send.at[j], tp_recv.at[j], z, xh, (t + j) % groups, r)

    rows_here = pl.ds(pl.multiple_of(r * half_units, half_units), half_units)

    def w_columns(to_t):
        return pl.ds(pl.multiple_of(to_t * width, width), width)

    def w_copy(j):
        to = (place + j) % (2 * groups)
        return push(
            base.at[rows_here, w_columns(to % groups)],
            weights.at[t * 2 + xh, rows_here, :],
            w_send.at[j], w_recv.at[j], z, to // groups, to % groups, r,
        )

    def pair_copy():
        return push(weights.at[:, rows_here, :], weights.at[:, rows_here, :], pair_send, pair_recv, z, xh, t, 1 - r)

    def code_copy():
        return push(codes.at[:, 1 - xh], swapped.at[xh], code_send, code_recv, z, 1 - xh, t, r)

    def right_copy(i):
        block = ring.at[(z - i + planes) % planes]
        return push(block, block, right_send.at[i], right_recv.at[i], (z + 1) % planes, xh, t, r)

    def left_copy(i):
        block = ring.at[(z + i) % planes]
        return push(block, block, left_send.at[i], left_recv.at[i], (z + planes - 1) % planes, xh, t, r)

    own_disp = pltpu.make_async_copy(disp.at[z], slots.at[t, z], local_sem.at[0])
    own_w = pltpu.make_async_copy(
        base.at[rows_here, w_columns(t)], weights.at[t * 2 + xh, rows_here, :], local_sem.at[1]
    )
    own_codes = pltpu.make_async_copy(codes.at[:, xh], swapped.at[xh], local_sem.at[2])
    own_quad = pltpu.make_async_copy(quarters.at[home], quad.at[home], local_sem.at[3])
    own_disp.start()
    own_w.start()
    own_codes.start()
    own_quad.start()
    pl.semaphore_wait(pltpu.get_barrier_semaphore(), (planes - 1) + (2 * groups - 1) + 2)

    for i in range(1, 4):
        quad_copy(i).start()
    loop(1, planes, lambda d: disp_copy(d).start())
    own_quad.wait()
    for i in range(1, 4):
        quad_copy(i).wait()
    part = quarters.shape[1] - 16
    for i in range(4):
        ring[z, i * part:(i + 1) * part, :] = quad[i, :part, :]
    ring[z, 4 * part:, :] = (
        quad[0, part:, :] + quad[1, part:, :] + quad[2, part:, :] + quad[3, part:, :]
    )
    right_copy(0).start()
    left_copy(0).start()
    loop(1, 2 * groups, lambda j: w_copy(j).start())
    code_copy().start()

    right_steps = planes // 2
    left_steps = planes - 1 - right_steps

    def ring_step(i):
        right_copy(i - 1).wait_recv()
        right_copy(i).start()
        left_copy(i - 1).wait_recv()
        left_copy(i).start()

    middle = left_steps // 2
    loop(1, middle, ring_step)
    own_disp.wait()
    loop(1, planes, lambda d: disp_copy(d).wait())
    loop(1, groups, lambda j: tp_copy(j).start())
    loop(middle, left_steps, ring_step)
    own_w.wait()
    loop(1, 2 * groups, lambda j: w_copy(j).wait())
    pair_copy().start()
    right_copy(left_steps - 1).wait_recv()
    right_copy(left_steps).start()
    left_copy(left_steps - 1).wait_recv()
    right_copy(left_steps).wait_recv()
    loop(0, right_steps, lambda i: right_copy(i).wait_send())
    loop(0, left_steps, lambda i: left_copy(i).wait_send())
    loop(1, groups, lambda j: tp_copy(j).wait())
    own_codes.wait()
    code_copy().wait()
    pair_copy().wait()


def code_kernel(per, ring_ref, weight_ref, out_ref, wide):
    block = ring_ref[...]
    rows = per * 64
    lanes = 128
    tags = block[:, 128:, :].reshape(per * 16, lanes)
    lane_in = lax.broadcasted_iota(jnp.int32, (lanes, 4 * lanes), 0)
    lane_out = lax.broadcasted_iota(jnp.int32, (lanes, 4 * lanes), 1)
    named = []
    for home in range(4):
        pick = jnp.where(lane_in == home * 32 + (lane_out // lanes) * 8, 1.0, 0.0).astype(BF16)
        spread = jnp.dot(tags, pick, preferred_element_type=F32)
        named.append(spread.reshape(per, 1, 16, 4 * lanes))
    named = jnp.concatenate(named, axis=1).reshape(rows, 4 * lanes)
    upper = jnp.where(lax.broadcasted_iota(jnp.int32, (rows, 4 * lanes), 1) % lanes >= 64, 1.0, 0.0)
    named = (named - upper).astype(BF16)
    lane_in = lax.broadcasted_iota(jnp.int32, (lanes, 2 * lanes), 0)
    lane_out = lax.broadcasted_iota(jnp.int32, (lanes, 2 * lanes), 1)
    double = jnp.where(lane_in == (lane_out // lanes) * 64 + lane_out % 64, 1.0, 0.0).astype(BF16)
    acts = block[:, :128, :].reshape(per, 4, 2, 16, lanes)
    values, names = [], []
    for m in range(2):
        both = jnp.dot(
            acts[:, :, m].reshape(rows, lanes), double, preferred_element_type=F32
        ).astype(BF16)
        for j in range(2):
            values.append(both[:, j * lanes:(j + 1) * lanes])
            names.append(named[:, (m * 2 + j) * lanes:(m * 2 + j + 1) * lanes])
    pairs = weight_ref.shape[0] // lanes
    for pair in range(pairs):
        chosen = jnp.zeros((rows, lanes), BF16)
        for value, name in zip(values, names):
            chosen = jnp.where(name == jnp.asarray(2.0 * pair, BF16), value, chosen)
        wide[:, pair * lanes:(pair + 1) * lanes] = chosen
    total = jnp.dot(wide[...], weight_ref[...], preferred_element_type=F32)
    cols = weight_ref.shape[1]
    total = total.reshape(per, 4, 2, 8, cols).sum(axis=2)
    for home in range(4):
        out_ref[0, home] = total[:, home].reshape(per * 8, cols).astype(BF16)


def return_kernel(
    planes, groups, base_out, code_out, base_in, code_in,
    gathered, total, local_sem, base_send, base_recv, plane_send, plane_recv, home_send, home_recv,
):
    z, xh, t, r = position()
    per = planes // groups
    me = (xh * groups + t) * 2 + r
    count = 4 * groups

    def hello(to_z, to_xh, to_t, to_r):
        pl.semaphore_signal(
            pltpu.get_barrier_semaphore(),
            inc=1,
            device_id=(to_z * 2 + to_xh, to_t, to_r),
            device_id_type=MESH,
        )

    loop(1, planes, lambda d: hello((z + d) % planes, xh, t, r))

    def place_of(j):
        other = (me + j) % count
        return other // (2 * groups), (other // 2) % groups, other % 2

    def hello_plane(j):
        to_xh, to_t, to_r = place_of(j)
        hello(z, to_xh, to_t, to_r)

    loop(1, count, hello_plane)
    stays = (z // per == t).astype(jnp.int32)

    def hello_source(j):
        @pl.when(jnp.logical_not(jnp.logical_and(z // per == t, z % per == j)))
        def _():
            hello(t * per + j, xh, z // per, r)

    for j in range(per):
        hello_source(j)

    def base_copy(d):
        to = (z + d) % planes
        return push(base_out.at[to], base_in.at[z], base_send.at[d], base_recv.at[d], to, xh, t, r)

    def plane_copy(j):
        to_xh, to_t, to_r = place_of(j)
        return push(
            code_out.at[to_t, to_xh * 2 + to_r], gathered.at[me],
            plane_send.at[j], plane_recv.at[j], z, to_xh, to_t, to_r,
        )

    def home_copy(i):
        return push(
            total.at[pl.ds(i * 8, 8), :], code_in.at[z % per],
            home_send.at[i], home_recv.at[z % per], t * per + i, xh, z // per, r,
        )

    def home_arrival(j):
        return push(
            total.at[pl.ds(j * 8, 8), :], code_in.at[j],
            home_send.at[j], home_recv.at[j], t * per + j, xh, z // per, r,
        )

    own_base = pltpu.make_async_copy(base_out.at[z], base_in.at[z], local_sem.at[0])
    own_code = pltpu.make_async_copy(code_out.at[t, xh * 2 + r], gathered.at[me], local_sem.at[1])
    own_base.start()
    own_code.start()
    pl.semaphore_wait(
        pltpu.get_barrier_semaphore(), (planes - 1) + (count - 1) + per - stays
    )
    loop(1, count, lambda j: plane_copy(j).start())
    loop(1, planes, lambda d: base_copy(d).start())
    own_code.wait()
    loop(1, count, lambda j: plane_copy(j).wait())

    def add(j, running):
        return running + gathered[j].astype(F32)

    total[...] = lax.fori_loop(0, count, add, jnp.zeros(total.shape, F32))
    for i in range(per):
        stay = jnp.logical_and(z // per == t, z % per == i)

        @pl.when(jnp.logical_not(stay))
        def _():
            home_copy(i).start()

        @pl.when(stay)
        def _():
            code_in[i] = total[i * 8:(i + 1) * 8, :]

    own_base.wait()
    loop(1, planes, lambda d: base_copy(d).wait())
    for i in range(per):
        stay = jnp.logical_and(z // per == t, z % per == i)

        @pl.when(jnp.logical_not(stay))
        def _():
            home_copy(i).wait_send()
            home_arrival(i).wait_recv()


def shards(base_weight, delta_codes, block_scales, hidden_acts, expert_ids, gate_weights):
    groups = lax.axis_size("tp")
    planes = lax.axis_size("fsdp") // 2
    steps, rows, top = expert_ids.shape
    units = hidden_acts.shape[4]
    width = base_weight.shape[2]
    narrow = delta_codes.shape[2]
    block_count = block_scales.shape[2]
    z, xh, t, r = position()
    capacity = 2
    slot_count = rows * top
    per = planes // groups

    flat_ids = expert_ids.reshape(steps, slot_count)
    slot_index = jnp.arange(slot_count, dtype=jnp.int32)
    earlier = (flat_ids[:, :, None] == flat_ids[:, None, :]) & (
        slot_index[None, None, :] < slot_index[None, :, None]
    )
    order = jnp.sum(earlier.astype(jnp.int32), axis=2)
    select = (
        flat_ids[:, None, None, :] == jnp.arange(planes, dtype=jnp.int32)[None, :, None, None]
    ) & (order[:, None, None, :] == jnp.arange(capacity, dtype=jnp.int32)[None, None, :, None])
    gated = (hidden_acts.astype(F32) * gate_weights[..., None, None]).astype(BF16)
    packed = jnp.einsum(
        "secj,sjph->epsch",
        select.astype(BF16),
        gated.reshape(steps, slot_count, 2, units),
        preferred_element_type=F32,
    ).astype(BF16).reshape(planes, 8, units)
    scales = block_scales.reshape(block_count)
    scale_high = lax.reduce_precision(scales, 8, 7)
    scale_rows = jnp.stack([scale_high, scales - scale_high]).astype(BF16)
    scale_rows = jnp.pad(scale_rows, ((0, 6), (0, units - block_count)))
    disp = jnp.concatenate(
        [packed, jnp.broadcast_to(scale_rows[None], (planes, 8, units))], axis=1
    )
    quarters = (
        gated.reshape(steps, rows, 2, 2, 2, 2, 2, 64)
        .transpose(5, 6, 3, 4, 0, 1, 2, 7)
        .reshape(4, 32, 128)
    )
    tags = expert_ids.reshape(steps, rows, 2, 2, 2).transpose(4, 0, 1, 3, 2).reshape(16, 4)
    tags = jnp.pad(tags.astype(BF16)[:, :, None], ((0, 0), (0, 0), (0, 7))).reshape(16, 1, 32)
    tags = jnp.where((jnp.arange(4) == xh * 2 + r)[None, :, None], tags, 0.0).reshape(1, 16, 128)
    quarters = jnp.concatenate([quarters, jnp.broadcast_to(tags, (4, 16, 128))], axis=1)

    dma = pltpu.SemaphoreType.DMA
    vmem = pl.BlockSpec(memory_space=pltpu.VMEM)
    anywhere = pl.BlockSpec(memory_space=pl.ANY)
    half = planes // 2

    def spread_body(*refs):
        spread_kernel(planes, groups, *refs)

    slots, ring, weights, swapped = pl.pallas_call(
        spread_body,
        out_shape=(
            jax.ShapeDtypeStruct((groups, planes, 16, 128), BF16),
            jax.ShapeDtypeStruct((planes, 144, 128), BF16),
            jax.ShapeDtypeStruct((2 * groups, units, width // groups), BF16),
            jax.ShapeDtypeStruct((2, planes, 64, narrow), BF16),
        ),
        in_specs=[vmem, vmem, anywhere, anywhere],
        out_specs=(vmem, vmem, anywhere, anywhere),
        scratch_shapes=[
            pltpu.VMEM((4, 48, 128), BF16),
            dma((4,)),
            dma((4,)), dma((4,)),
            dma((planes,)), dma((planes,)),
            dma((groups,)), dma((groups,)),
            dma((2 * groups,)), dma((2 * groups,)),
            dma, dma, dma, dma,
            dma((half,)), dma((half,)), dma((half,)), dma((half,)),
        ],
        compiler_params=pltpu.CompilerParams(
            collective_id=0, has_side_effects=True, vmem_limit_bytes=32 << 20
        ),
    )(disp, quarters, base_weight.reshape(units, width), delta_codes.reshape(planes, 2, 64, narrow))

    held_scales = lax.dynamic_index_in_dim(slots, t, 0, keepdims=False)[:, 8:10, :block_count].astype(F32)
    held_scales = held_scales[:, 0] + held_scales[:, 1]
    column = (2 * z + jnp.arange(2, dtype=jnp.int32)[:, None]) * narrow + jnp.arange(narrow, dtype=jnp.int32)[None, :]
    spot = (column // (width // block_count))[:, None, :] == jnp.arange(block_count, dtype=jnp.int32)[None, :, None]
    column_scales = jnp.einsum(
        "eb,xbc->xec", held_scales, spot.astype(F32), precision=lax.Precision.HIGHEST
    )
    scaled = (swapped.astype(F32) * column_scales[:, :, None, :]).astype(BF16)
    scaled = jnp.pad(scaled, ((0, 0), (0, 0), (0, 0), (0, 128 - narrow)))
    scaled = jnp.concatenate([scaled[0], scaled[1]], axis=2).reshape(planes * 64, 256)
    code_out = pl.pallas_call(
        lambda *refs: code_kernel(per, *refs),
        grid=(groups,),
        out_shape=jax.ShapeDtypeStruct((groups, 4, per * 8, 256), BF16),
        in_specs=[
            pl.BlockSpec((per, 144, 128), lambda g: (g, 0, 0)),
            pl.BlockSpec((planes * 64, 256), lambda g: (0, 0)),
        ],
        out_specs=pl.BlockSpec((1, 4, per * 8, 256), lambda g: (g, 0, 0, 0)),
        scratch_shapes=[pltpu.VMEM((per * 64, planes * 64), BF16)],
        compiler_params=pltpu.CompilerParams(vmem_limit_bytes=32 << 20),
    )(ring, scaled)

    acts = (
        slots[:, :, :8, :]
        .reshape(groups, planes, 2, 4, units)
        .transpose(1, 3, 0, 2, 4)
        .reshape(planes * 4, groups * 2 * units)
    )
    projected = jnp.dot(
        acts, weights.reshape(groups * 2 * units, width // groups), preferred_element_type=F32
    ).astype(BF16)
    lines = 4 * (width // groups) // 128
    base_out = jnp.pad(projected.reshape(planes, lines, 128), ((0, 0), (0, 32 - lines), (0, 0)))

    def return_body(*refs):
        return_kernel(planes, groups, *refs)

    base_in, code_in = pl.pallas_call(
        return_body,
        out_shape=(
            jax.ShapeDtypeStruct((planes, 32, 128), BF16),
            jax.ShapeDtypeStruct((per, 8, 256), F32),
        ),
        in_specs=[vmem, vmem],
        out_specs=(vmem, vmem),
        scratch_shapes=[
            pltpu.VMEM((4 * groups, per * 8, 256), BF16),
            pltpu.VMEM((per * 8, 256), F32),
            dma((2,)),
            dma((planes,)), dma((planes,)),
            dma((4 * groups,)), dma((4 * groups,)),
            dma((per,)), dma((per,)),
        ],
        compiler_params=pltpu.CompilerParams(
            collective_id=1, has_side_effects=True, vmem_limit_bytes=32 << 20
        ),
    )(base_out, code_out)

    back = base_in[:, :lines].reshape(planes, steps, capacity, width // groups)
    row_select = select.reshape(steps, planes, capacity, rows, top).astype(F32).sum(axis=4).astype(BF16)
    mixed = jnp.einsum("secn,escd->snd", row_select, back, preferred_element_type=F32)
    coded = (
        code_in.reshape(per, steps, rows, 2, 128)[..., :narrow]
        .transpose(1, 2, 0, 3, 4)
        .reshape(steps, rows, width // groups)
    )
    return (mixed + coded).astype(BF16)


def solution(mesh):
    placed = (
        P("fsdp", "tp", None),
        P(None, ("tp", "rep"), "fsdp"),
        P("fsdp", "tp", None),
        P(None, ("fsdp", "rep"), None, None, "tp"),
        P(None, ("fsdp", "rep"), None),
        P(None, ("fsdp", "rep"), None),
    )
    return jax.shard_map(
        shards,
        mesh=mesh,
        in_specs=placed,
        out_specs=P(None, ("fsdp", "rep"), "tp"),
        check_vma=False,
    )
```

```python
import jax
import jax.numpy as jnp
from jax import lax
from jax.experimental import pallas as pl
from jax.experimental.pallas import tpu as pltpu
from jax.sharding import PartitionSpec as P

MESH = pl.DeviceIdType.MESH
BF16 = jnp.bfloat16
F32 = jnp.float32


def position():
    f, t, r = lax.axis_index("fsdp"), lax.axis_index("tp"), lax.axis_index("rep")
    return f // 2, f % 2, t, r


def push(src, dst, send_sem, recv_sem, z, xh, t, r):
    return pltpu.make_async_remote_copy(
        src_ref=src,
        dst_ref=dst,
        send_sem=send_sem,
        recv_sem=recv_sem,
        device_id=(z * 2 + xh, t, r),
        device_id_type=MESH,
    )


def loop(low, high, body):
    def step(i, carry):
        body(i)
        return carry

    lax.fori_loop(low, high, step, jnp.int32(0))


def iota(shape, axis):
    return lax.broadcasted_iota(jnp.int32, shape, axis)


def one_hot(condition):
    return jnp.where(condition, 1.0, 0.0).astype(BF16)


STRIDE = 2


def resync_kernel(
    planes, groups, hidden, ids, gate_weights, scales, base, codes,
    base_in, code_in,
    scale_rows, disp, quarters, quad, slots, ring, weights, swapped, column_scales, wide_weights, wide,
    acts, base_out, code_out, gathered, total,
    local_sem, quad_send, quad_recv, disp_send, disp_recv, tp_send, tp_recv,
    w_send, w_recv, pair_send, pair_recv, code_send, code_recv,
    right_send, right_recv, left_send, left_recv,
    base_send, base_recv, plane_send, plane_recv, home_send, home_recv,
):
    z, xh, t, r = position()
    home = xh * 2 + r
    place = xh * groups + t
    me = place * 2 + r
    count = 4 * groups
    per = planes // groups
    half_units = base.shape[0] // 2
    width = weights.shape[2]
    narrow = codes.shape[3]
    lanes = 128

    def hello(to_z, to_xh, to_t, to_r):
        pl.semaphore_signal(
            pltpu.get_barrier_semaphore(),
            inc=1,
            device_id=(to_z * 2 + to_xh, to_t, to_r),
            device_id_type=MESH,
        )

    def place_of(j):
        other = (me + j) % count
        return other // (2 * groups), (other // 2) % groups, other % 2

    def hello_plane(j):
        to_xh, to_t, to_r = place_of(j)
        hello(z, to_xh, to_t, to_r)

    def stays(i):
        return jnp.logical_and(z // per == t, z % per == i)

    loop(1, planes, lambda d: hello((z + d) % planes, xh, t, r))
    loop(1, count, hello_plane)
    for j in range(per):
        @pl.when(jnp.logical_not(stays(j)))
        def _():
            hello(t * per + j, xh, z // per, r)

    def quad_copy(i):
        to = (home + i) % 4
        return push(quarters.at[to], quad.at[home], quad_send.at[i], quad_recv.at[i], z, to // 2, t, to % 2)

    def disp_copy(d):
        to = (z + d) % planes
        return push(disp.at[to], slots.at[z], disp_send.at[d], disp_recv.at[d], to, xh, t, r)

    def tp_copy(j):
        return push(acts.at[t], acts.at[t], tp_send.at[j], tp_recv.at[j], z, xh, (t + j) % groups, r)

    rows_here = pl.ds(pl.multiple_of(r * half_units, half_units), half_units)

    def w_columns(to_t):
        return pl.ds(pl.multiple_of(to_t * width, lanes), width)

    def w_copy(j):
        to = (place + j) % (2 * groups)
        return push(
            base.at[rows_here, w_columns(to % groups)], weights.at[place, rows_here, :],
            w_send.at[j], w_recv.at[j], z, to // groups, to % groups, r,
        )

    def pair_copy(j):
        block = weights.at[(place + 2 * groups - j) % (2 * groups), rows_here, :]
        return push(block, block, pair_send.at[j], pair_recv.at[j], z, xh, t, 1 - r)

    def code_copy():
        return push(codes.at[:, 1 - xh], swapped.at[xh], code_send, code_recv, z, 1 - xh, t, r)

    def right_block(o):
        return ring.at[(z - o + planes) % planes]

    def left_block(o):
        return ring.at[(z + o) % planes]

    def right_seed(d):
        return push(ring.at[z], ring.at[z], right_send.at[d], right_recv.at[d], (z + d) % planes, xh, t, r)

    def left_seed(d):
        return push(ring.at[z], ring.at[z], left_send.at[d], left_recv.at[d], (z + planes - d) % planes, xh, t, r)

    def right_next(o):
        return push(
            right_block(o), right_block(o), right_send.at[o + STRIDE], right_recv.at[o + STRIDE],
            (z + STRIDE) % planes, xh, t, r,
        )

    def left_next(o):
        return push(
            left_block(o), left_block(o), left_send.at[o + STRIDE], left_recv.at[o + STRIDE],
            (z + planes - STRIDE) % planes, xh, t, r,
        )

    def right_wait(o):
        push(right_block(o), right_block(o), right_send.at[o], right_recv.at[o], z ^ 1, xh, t, r).wait_recv()

    def left_wait(o):
        push(left_block(o), left_block(o), left_send.at[o], left_recv.at[o], z ^ 1, xh, t, r).wait_recv()

    right_last = planes // 2
    left_last = planes - 1 - right_last

    def ring_steps(low, high):
        def step(o):
            right_wait(o)
            right_next(o).start()
            left_wait(o)
            left_next(o).start()

        loop(low, high, step)

    def base_copy(d):
        to = (z + d) % planes
        return push(base_out.at[to], base_in.at[z], base_send.at[d], base_recv.at[d], to, xh, t, r)

    def plane_copy(j):
        to_xh, to_t, to_r = place_of(j)
        return push(
            code_out.at[to_t, to_xh * 2 + to_r], gathered.at[me],
            plane_send.at[j], plane_recv.at[j], z, to_xh, to_t, to_r,
        )

    def home_copy(i):
        return push(
            total.at[pl.ds(i * 8, 8), :], code_in.at[z % per],
            home_send.at[i], home_recv.at[z % per], t * per + i, xh, z // per, r,
        )

    def home_arrival(j):
        return push(
            total.at[pl.ds(j * 8, 8), :], code_in.at[j],
            home_send.at[j], home_recv.at[j], t * per + j, xh, z // per, r,
        )

    own_w = pltpu.make_async_copy(
        base.at[rows_here, w_columns(t)], weights.at[place, rows_here, :], local_sem.at[0]
    )
    own_codes = pltpu.make_async_copy(codes.at[:, xh], swapped.at[xh], local_sem.at[1])
    own_w.start()
    own_codes.start()

    square = (lanes, lanes)
    def column_of(values):
        tall = jnp.broadcast_to(values[:, None, :], (8, 16, 8)).reshape(lanes, 8)
        mine = iota((lanes, 8), 1) == iota((lanes, 8), 0) // 2 % 8
        return jnp.sum(jnp.where(mine, tall, 0.0), axis=1, keepdims=True)

    gated = (hidden[...].astype(F32) * column_of(gate_weights[...])).astype(BF16)
    names_column = jnp.broadcast_to(column_of(ids[...].astype(F32)), square)
    row, col = iota(square, 0), iota(square, 1)
    wanted = (
        ((row // 4) % 2 * 4 + row % 4) * 16 + (row // 32 % 2) * 8 + (row // 16 % 2) * 4
        + (row // 8 % 2) * 2 + row // 64
    )
    sorted_rows = jnp.dot(one_hot(col == wanted), gated, preferred_element_type=F32).astype(BF16)
    for half in range(2):
        low = sorted_rows[half * 64:half * 64 + 32, :]
        high = sorted_rows[half * 64 + 32:half * 64 + 64, :]
        quarters[half * 2, 0:32, :] = jnp.concatenate([low[:, :64], high[:, :64]], axis=1)
        quarters[half * 2 + 1, 0:32, :] = jnp.concatenate([low[:, 64:], high[:, 64:]], axis=1)
    named = jnp.sum(jnp.where(row == col, names_column, 0.0), axis=0, keepdims=True)
    tag_shape = (16, lanes)
    tag_row, tag_col = iota(tag_shape, 0), iota(tag_shape, 1)
    tag_at = (
        ((tag_row // 4) % 2 * 4 + tag_row % 4 == tag_col // 16)
        & (tag_row // 8 == tag_col // 2 % 2) & (tag_col % 2 == 0)
    )
    tag_values = jnp.where(tag_at, jnp.broadcast_to(named, tag_shape), 0.0).astype(BF16)
    tag_lane = home * 32 + ((row // 4 % 2) * 2 + row // 8 % 2) * 8
    tags = jnp.dot(tag_values, one_hot(col == tag_lane), preferred_element_type=F32).astype(BF16)
    for i in range(4):
        quarters[i, 32:48, :] = tags
    same = (
        (names_column == named) & (row < col) & (row % 2 == col % 2) & (row // 64 == col // 64)
    )
    order = jnp.sum(jnp.where(same, 1.0, 0.0), axis=0, keepdims=True)
    pack_shape = (planes * 8, lanes)
    pack_row, pack_col = iota(pack_shape, 0), iota(pack_shape, 1)
    picked = (
        (jnp.broadcast_to(named, pack_shape) == (pack_row // 8).astype(F32))
        & (jnp.broadcast_to(order, pack_shape) == (pack_row % 2).astype(F32))
        & (pack_row // 2 % 2 == pack_col // 64) & (pack_row // 4 % 2 == pack_col % 2)
    )
    packed = jnp.dot(one_hot(picked), gated, preferred_element_type=F32).reshape(planes, 8, lanes)
    blocks = scales.shape[1]
    high = scales[...].astype(BF16).astype(F32)
    scale_rows[...] = jnp.zeros(scale_rows.shape, F32)
    scale_rows[0:1, :blocks] = high
    scale_rows[1:2, :blocks] = scales[...] - high
    disp[...] = jnp.concatenate(
        [packed, jnp.broadcast_to(scale_rows[...][None], (planes, 8, lanes))], axis=1
    ).astype(BF16)
    wide_weights[...] = jnp.zeros(wide_weights.shape, BF16)
    pl.semaphore_wait(
        pltpu.get_barrier_semaphore(),
        (planes - 1) + (count - 1) + per - (z // per == t).astype(jnp.int32),
    )

    for i in range(1, 4):
        quad_copy(i).start()
    loop(1, 2 * groups, lambda j: w_copy(j).start())
    code_copy().start()
    quad[home] = quarters[home]
    for i in range(1, 4):
        quad_copy(i).wait()
    for i in range(4):
        ring[z, i * 32:(i + 1) * 32, :] = quad[i, :32, :]
    ring[z, 128:, :] = quad[0, 32:, :] + quad[1, 32:, :] + quad[2, 32:, :] + quad[3, 32:, :]
    for d in range(1, STRIDE + 1):
        right_seed(d).start()
        left_seed(d).start()
    loop(1, planes, lambda d: disp_copy(d).start())
    slots[z] = disp[z]

    def code_group(index):
        g = (z // per + ((index + 1) // 2) * (2 * (index % 2) - 1) + groups) % groups
        block = ring[pl.ds(g * per, per)]
        rows = per * 64
        tag_block = block[:, 128:, :].reshape(per * 16, lanes)
        lane_in, lane_out = iota((lanes, 4 * lanes), 0), iota((lanes, 4 * lanes), 1)
        names = []
        for h in range(4):
            pick = one_hot(lane_in == h * 32 + (lane_out // lanes) * 8)
            spread = jnp.dot(tag_block, pick, preferred_element_type=F32)
            names.append(spread.reshape(per, 1, 16, 4 * lanes))
        names = jnp.concatenate(names, axis=1).reshape(rows, 4 * lanes)
        upper = jnp.where(iota((rows, 4 * lanes), 1) % lanes >= 64, 1.0, 0.0)
        names = (names - upper).astype(BF16)
        lane_in, lane_out = iota((lanes, 2 * lanes), 0), iota((lanes, 2 * lanes), 1)
        double = one_hot(lane_in == (lane_out // lanes) * 64 + lane_out % 64)
        parts = block[:, :128, :].reshape(per, 4, 2, 16, lanes)
        values, tagged = [], []
        for m in range(2):
            both = jnp.dot(
                parts[:, :, m].reshape(rows, lanes), double, preferred_element_type=F32
            ).astype(BF16)
            for j in range(2):
                values.append(both[:, j * lanes:(j + 1) * lanes])
                tagged.append(names[:, (m * 2 + j) * lanes:(m * 2 + j + 1) * lanes])
        for pair in range(planes // 2):
            chosen = jnp.zeros((rows, lanes), BF16)
            for value, name in zip(values, tagged):
                chosen = jnp.where(name == jnp.asarray(2.0 * pair, BF16), value, chosen)
            wide[:, pair * lanes:(pair + 1) * lanes] = chosen
        result = jnp.dot(wide[...], wide_weights[...], preferred_element_type=F32)
        cols = wide_weights.shape[1]
        result = result.reshape(per, 4, 2, 8, cols).sum(axis=2)
        for h in range(4):
            code_out[g, h] = result[:, h].reshape(per * 8, cols).astype(BF16)
        for h in range(4):
            to = ((h // 2) * groups + g) * 2 + h % 2
            leaves = to != me

            @pl.when(leaves)
            def _():
                plane_copy((to - me + count) % count).start()

            @pl.when(jnp.logical_not(leaves))
            def _():
                gathered[me] = code_out[g, h]

    ring_steps(1, 9)
    loop(1, planes, lambda d: disp_copy(d).wait())
    acts[t] = slots[...].astype(F32)[:, :8, :].reshape(planes * 8, lanes).astype(BF16)
    loop(1, groups, lambda j: tp_copy(j).start())
    ring_steps(9, 10)

    own_codes.wait()
    code_copy().wait()
    spot_in, spot_out = iota((lanes, 2 * lanes), 0), iota((lanes, 2 * lanes), 1)
    column = (2 * z + spot_out // lanes) * narrow + spot_out % lanes
    spot = one_hot((column // lanes == spot_in) & (spot_out % lanes < narrow))
    spread = jnp.dot(
        slots[...].reshape(planes * 16, lanes), spot, preferred_element_type=F32
    ).reshape(planes, 16, 2 * lanes)
    column_scales[...] = spread[:, 8:9, :] + spread[:, 9:10, :]

    def scale_expert(e):
        at = pl.ds(pl.multiple_of(e * 64, 64), 64)
        for x in range(2):
            scale = column_scales[e, :, x * lanes:x * lanes + narrow]
            wide_weights[at, x * lanes:x * lanes + narrow] = (
                swapped[x, e].astype(F32) * scale
            ).astype(BF16)

    loop(0, planes, scale_expert)
    ring_steps(10, 11)
    loop(0, 1, code_group)
    ring_steps(11, 12)
    own_w.wait()
    pair_copy(0).start()

    def pass_on(j):
        w_copy(j).wait_recv()
        pair_copy(j).start()

    loop(1, 2 * groups, pass_on)
    ring_steps(12, 13)
    loop(1, 3, code_group)
    ring_steps(13, left_last - STRIDE + 1)
    for o in range(left_last - STRIDE + 1, right_last - STRIDE + 1):
        right_wait(o)
        right_next(o).start()

    loop(1, groups, lambda j: tp_copy(j).wait())
    loop(0, 2 * groups, lambda j: pair_copy(j).wait())
    left = jnp.concatenate([acts[g] for g in range(groups)], axis=1)
    first = iota((planes, 8, lanes), 1) < 4
    lines = []
    for c in range(0, width, 2 * lanes):
        wide_cols = min(2 * lanes, width - c)
        zero, one = [
            jnp.dot(
                left,
                weights[p * groups:(p + 1) * groups, :, c:c + wide_cols].reshape(groups * lanes, wide_cols),
                preferred_element_type=F32,
            ).reshape(planes, 8, wide_cols)
            for p in range(2)
        ]
        blank = jnp.zeros((planes, 8, lanes), F32)
        zero_next, one_next = (zero[:, :, lanes:], one[:, :, lanes:]) if wide_cols > lanes else (blank, blank)
        stay = jnp.where(first, zero[:, :, :lanes], one_next)
        move = jnp.where(first, zero_next, one[:, :, :lanes])
        lines.append(stay + pltpu.roll(move, 4, 1))
    base_out[...] = jnp.concatenate(lines, axis=1).astype(BF16)
    loop(1, planes, lambda d: base_copy(d).start())
    base_in[z] = base_out[z]

    loop(3, 5, code_group)
    for o in range(right_last - STRIDE + 1, right_last + 1):
        right_wait(o)
    for o in range(left_last - STRIDE + 1, left_last + 1):
        left_wait(o)
    loop(5, groups, code_group)

    loop(1, count, lambda j: plane_copy(j).wait())

    def add(j, running):
        return running + gathered[j].astype(F32)

    total[...] = lax.fori_loop(0, count, add, jnp.zeros(total.shape, F32))
    for i in range(per):
        @pl.when(jnp.logical_not(stays(i)))
        def _():
            home_copy(i).start()

        @pl.when(stays(i))
        def _():
            code_in[i] = total[i * 8:(i + 1) * 8, :]

    loop(1, 2 * groups, lambda j: w_copy(j).wait_send())
    for d in range(1, STRIDE + 1):
        right_seed(d).wait_send()
        left_seed(d).wait_send()
    loop(1, right_last - STRIDE + 1, lambda o: right_next(o).wait_send())
    loop(1, left_last - STRIDE + 1, lambda o: left_next(o).wait_send())
    loop(1, planes, lambda d: base_copy(d).wait())
    for i in range(per):
        @pl.when(jnp.logical_not(stays(i)))
        def _():
            home_copy(i).wait_send()
            home_arrival(i).wait_recv()


def shards(base_weight, delta_codes, block_scales, hidden_acts, expert_ids, gate_weights):
    groups = lax.axis_size("tp")
    planes = lax.axis_size("fsdp") // 2
    steps, rows, top = expert_ids.shape
    units = hidden_acts.shape[4]
    width = base_weight.shape[2]
    narrow = delta_codes.shape[2]
    block_count = block_scales.shape[2]
    capacity = 2
    slot_count = rows * top
    per = planes // groups
    total_slots = steps * slot_count

    dma = pltpu.SemaphoreType.DMA
    vmem = pl.BlockSpec(memory_space=pltpu.VMEM)
    outside = pl.BlockSpec(memory_space=pltpu.HBM)
    count = 4 * groups

    def body(*refs):
        resync_kernel(planes, groups, *refs)

    base_in, code_in = pl.pallas_call(
        body,
        out_shape=(
            jax.ShapeDtypeStruct((planes, 32, 128), BF16),
            jax.ShapeDtypeStruct((per, 8, 256), F32),
        ),
        in_specs=[vmem, vmem, vmem, vmem, outside, outside],
        out_specs=(vmem, vmem),
        scratch_shapes=[
            pltpu.VMEM((8, 128), F32),
            pltpu.VMEM((planes, 16, 128), BF16),
            pltpu.VMEM((4, 48, 128), BF16),
            pltpu.VMEM((4, 48, 128), BF16),
            pltpu.VMEM((planes, 16, 128), BF16),
            pltpu.VMEM((planes, 144, 128), BF16),
            pltpu.VMEM((2 * groups, units, width // groups), BF16),
            pltpu.VMEM((2, planes, 64, narrow), BF16),
            pltpu.VMEM((planes, 1, 256), F32),
            pltpu.VMEM((planes * 64, 256), BF16),
            pltpu.VMEM((per * 64, planes * 64), BF16),
            pltpu.VMEM((groups, planes * 8, units), BF16),
            pltpu.VMEM((planes, 32, 128), BF16),
            pltpu.VMEM((groups, 4, per * 8, 256), BF16),
            pltpu.VMEM((count, per * 8, 256), BF16),
            pltpu.VMEM((per * 8, 256), F32),
            dma((2,)),
            dma((4,)), dma((4,)),
            dma((planes,)), dma((planes,)),
            dma((groups,)), dma((groups,)),
            dma((2 * groups,)), dma((2 * groups,)),
            dma((2 * groups,)), dma((2 * groups,)),
            dma, dma,
            dma((planes,)), dma((planes,)), dma((planes,)), dma((planes,)),
            dma((planes,)), dma((planes,)),
            dma((count,)), dma((count,)),
            dma((per,)), dma((per,)),
        ],
        compiler_params=pltpu.CompilerParams(
            collective_id=0, has_side_effects=True, vmem_limit_bytes=40 << 20
        ),
    )(
        hidden_acts.reshape(total_slots * 2, units),
        expert_ids.reshape(steps * rows, top),
        gate_weights.reshape(steps * rows, top),
        block_scales.reshape(1, block_count),
        base_weight.reshape(units, width),
        delta_codes.reshape(planes, 2, 64, narrow),
    )

    flat_ids = expert_ids.reshape(steps, slot_count)
    slot_index = jnp.arange(slot_count, dtype=jnp.int32)
    earlier = (flat_ids[:, :, None] == flat_ids[:, None, :]) & (
        slot_index[None, None, :] < slot_index[None, :, None]
    )
    order = jnp.sum(earlier.astype(jnp.int32), axis=2)
    select = (
        flat_ids[:, None, None, :] == jnp.arange(planes, dtype=jnp.int32)[None, :, None, None]
    ) & (order[:, None, None, :] == jnp.arange(capacity, dtype=jnp.int32)[None, None, :, None])
    row_select = select.reshape(steps, planes, capacity, rows, top).astype(F32).sum(axis=4).astype(BF16)
    blocks = width // groups // 128
    back = base_in[:, :4 * blocks].reshape(planes, blocks, steps, capacity, 128)
    mixed = jnp.einsum("secn,ebscl->snbl", row_select, back, preferred_element_type=F32)
    coded = (
        code_in.reshape(per, steps, rows, 2, 128)[..., :narrow]
        .transpose(1, 2, 0, 3, 4)
        .reshape(steps, rows, width // groups)
    )
    return (mixed.reshape(steps, rows, width // groups) + coded).astype(BF16)


def solution(mesh):
    placed = (
        P("fsdp", "tp", None),
        P(None, ("tp", "rep"), "fsdp"),
        P("fsdp", "tp", None),
        P(None, ("fsdp", "rep"), None, None, "tp"),
        P(None, ("fsdp", "rep"), None),
        P(None, ("fsdp", "rep"), None),
    )
    return jax.shard_map(
        shards,
        mesh=mesh,
        in_specs=placed,
        out_specs=P(None, ("fsdp", "rep"), "tp"),
        check_vma=False,
    )
```

```python
import jax
import jax.numpy as jnp
from jax import lax
from jax.experimental import pallas as pl
from jax.experimental.pallas import tpu as pltpu
from jax.sharding import PartitionSpec as P

MESH = pl.DeviceIdType.MESH
BF16 = jnp.bfloat16
F32 = jnp.float32


def position():
    f, t, r = lax.axis_index("fsdp"), lax.axis_index("tp"), lax.axis_index("rep")
    return f // 2, f % 2, t, r


def push(src, dst, send_sem, recv_sem, z, xh, t, r):
    return pltpu.make_async_remote_copy(
        src_ref=src,
        dst_ref=dst,
        send_sem=send_sem,
        recv_sem=recv_sem,
        device_id=(z * 2 + xh, t, r),
        device_id_type=MESH,
    )


def loop(low, high, body):
    def step(i, carry):
        body(i)
        return carry

    lax.fori_loop(low, high, step, jnp.int32(0))


def iota(shape, axis):
    return lax.broadcasted_iota(jnp.int32, shape, axis)


def one_hot(condition):
    return jnp.where(condition, 1.0, 0.0).astype(BF16)


STRIDE = 2


def resync_kernel(
    planes, groups, hidden, ids, gate_weights, scales, base, codes,
    base_in, code_in,
    scale_rows, disp, quarters, quad, slots, ring, weights, swapped, column_scales, wide_weights, wide,
    acts, base_out, code_out, gathered, total,
    local_sem, quad_send, quad_recv, disp_send, disp_recv, tp_send, tp_recv,
    w_send, w_recv, pair_send, pair_recv, code_send, code_recv,
    right_send, right_recv, left_send, left_recv,
    base_send, base_recv, plane_send, plane_recv, home_send, home_recv,
):
    z, xh, t, r = position()
    home = xh * 2 + r
    place = xh * groups + t
    me = place * 2 + r
    count = 4 * groups
    per = planes // groups
    half_units = base.shape[0] // 2
    width = weights.shape[2]
    narrow = codes.shape[3]
    lanes = 128

    def hello(to_z, to_xh, to_t, to_r):
        pl.semaphore_signal(
            pltpu.get_barrier_semaphore(),
            inc=1,
            device_id=(to_z * 2 + to_xh, to_t, to_r),
            device_id_type=MESH,
        )

    def place_of(j):
        other = (me + j) % count
        return other // (2 * groups), (other // 2) % groups, other % 2

    def hello_plane(j):
        to_xh, to_t, to_r = place_of(j)
        hello(z, to_xh, to_t, to_r)

    def stays(i):
        return jnp.logical_and(z // per == t, z % per == i)

    far = planes // 2

    def hello_both(i):
        hello((z + far + i) % planes, xh, t, r)
        hello((z + far - i + planes) % planes, xh, t, r)

    hello((z + far) % planes, xh, t, r)
    loop(1, far, hello_both)
    loop(1, count, hello_plane)
    for j in range(per):
        @pl.when(jnp.logical_not(stays(j)))
        def _():
            hello(t * per + j, xh, z // per, r)

    def quad_copy(i):
        to = (home + i) % 4
        return push(quarters.at[to], quad.at[home], quad_send.at[i], quad_recv.at[i], z, to // 2, t, to % 2)

    def disp_copy(d):
        to = (z + d) % planes
        return push(disp.at[to], slots.at[z], disp_send.at[d], disp_recv.at[d], to, xh, t, r)

    def tp_copy(j):
        return push(acts.at[t], acts.at[t], tp_send.at[j], tp_recv.at[j], z, xh, (t + j) % groups, r)

    rows_here = pl.ds(pl.multiple_of(r * half_units, half_units), half_units)

    def w_columns(to_t):
        return pl.ds(pl.multiple_of(to_t * width, lanes), width)

    def w_copy(j):
        to = (place + j) % (2 * groups)
        return push(
            base.at[rows_here, w_columns(to % groups)], weights.at[place, rows_here, :],
            w_send.at[j], w_recv.at[j], z, to // groups, to % groups, r,
        )

    def pair_copy(j):
        block = weights.at[(place + 2 * groups - j) % (2 * groups), rows_here, :]
        return push(block, block, pair_send.at[j], pair_recv.at[j], z, xh, t, 1 - r)

    def code_copy():
        return push(codes.at[:, 1 - xh], swapped.at[xh], code_send, code_recv, z, 1 - xh, t, r)

    def right_block(o):
        return ring.at[(z - o + planes) % planes]

    def left_block(o):
        return ring.at[(z + o) % planes]

    def right_seed(d):
        return push(ring.at[z], ring.at[z], right_send.at[d], right_recv.at[d], (z + d) % planes, xh, t, r)

    def left_seed(d):
        return push(ring.at[z], ring.at[z], left_send.at[d], left_recv.at[d], (z + planes - d) % planes, xh, t, r)

    def right_next(o):
        return push(
            right_block(o), right_block(o), right_send.at[o + STRIDE], right_recv.at[o + STRIDE],
            (z + STRIDE) % planes, xh, t, r,
        )

    def left_next(o):
        return push(
            left_block(o), left_block(o), left_send.at[o + STRIDE], left_recv.at[o + STRIDE],
            (z + planes - STRIDE) % planes, xh, t, r,
        )

    def right_wait(o):
        push(right_block(o), right_block(o), right_send.at[o], right_recv.at[o], z ^ 1, xh, t, r).wait_recv()

    def left_wait(o):
        push(left_block(o), left_block(o), left_send.at[o], left_recv.at[o], z ^ 1, xh, t, r).wait_recv()

    right_last = planes // 2
    left_last = planes - 1 - right_last

    def ring_steps(low, high):
        def step(o):
            right_wait(o)
            right_next(o).start()
            left_wait(o)
            left_next(o).start()

        loop(low, high, step)

    def base_copy(d):
        to = (z + d) % planes
        return push(base_out.at[to], base_in.at[z], base_send.at[d], base_recv.at[d], to, xh, t, r)

    def plane_copy(j):
        to_xh, to_t, to_r = place_of(j)
        return push(
            code_out.at[to_t, to_xh * 2 + to_r], gathered.at[me],
            plane_send.at[j], plane_recv.at[j], z, to_xh, to_t, to_r,
        )

    def home_copy(i):
        return push(
            total.at[pl.ds(i * 8, 8), :], code_in.at[z % per],
            home_send.at[i], home_recv.at[z % per], t * per + i, xh, z // per, r,
        )

    def home_arrival(j):
        return push(
            total.at[pl.ds(j * 8, 8), :], code_in.at[j],
            home_send.at[j], home_recv.at[j], t * per + j, xh, z // per, r,
        )

    own_w = pltpu.make_async_copy(
        base.at[rows_here, w_columns(t)], weights.at[place, rows_here, :], local_sem.at[0]
    )
    own_codes = pltpu.make_async_copy(codes.at[:, xh], swapped.at[xh], local_sem.at[1])
    own_w.start()
    own_codes.start()

    square = (lanes, lanes)
    def column_of(values):
        tall = jnp.broadcast_to(values[:, None, :], (8, 16, 8)).reshape(lanes, 8)
        mine = iota((lanes, 8), 1) == iota((lanes, 8), 0) // 2 % 8
        return jnp.sum(jnp.where(mine, tall, 0.0), axis=1, keepdims=True)

    gated = (hidden[...].astype(F32) * column_of(gate_weights[...])).astype(BF16)
    names_column = jnp.broadcast_to(column_of(ids[...].astype(F32)), square)
    row, col = iota(square, 0), iota(square, 1)
    wanted = (
        ((row // 4) % 2 * 4 + row % 4) * 16 + (row // 32 % 2) * 8 + (row // 16 % 2) * 4
        + (row // 8 % 2) * 2 + row // 64
    )
    sorted_rows = jnp.dot(one_hot(col == wanted), gated, preferred_element_type=F32).astype(BF16)
    for half in range(2):
        low = sorted_rows[half * 64:half * 64 + 32, :]
        high = sorted_rows[half * 64 + 32:half * 64 + 64, :]
        quarters[half * 2, 0:32, :] = jnp.concatenate([low[:, :64], high[:, :64]], axis=1)
        quarters[half * 2 + 1, 0:32, :] = jnp.concatenate([low[:, 64:], high[:, 64:]], axis=1)
    named = jnp.sum(jnp.where(row == col, names_column, 0.0), axis=0, keepdims=True)
    tag_shape = (16, lanes)
    tag_row, tag_col = iota(tag_shape, 0), iota(tag_shape, 1)
    tag_at = (
        ((tag_row // 4) % 2 * 4 + tag_row % 4 == tag_col // 16)
        & (tag_row // 8 == tag_col // 2 % 2) & (tag_col % 2 == 0)
    )
    tag_values = jnp.where(tag_at, jnp.broadcast_to(named, tag_shape), 0.0).astype(BF16)
    tag_lane = home * 32 + ((row // 4 % 2) * 2 + row // 8 % 2) * 8
    tags = jnp.dot(tag_values, one_hot(col == tag_lane), preferred_element_type=F32).astype(BF16)
    for i in range(4):
        quarters[i, 32:48, :] = tags
    same = (
        (names_column == named) & (row < col) & (row % 2 == col % 2) & (row // 64 == col // 64)
    )
    order = jnp.sum(jnp.where(same, 1.0, 0.0), axis=0, keepdims=True)
    pack_shape = (planes * 8, lanes)
    pack_row, pack_col = iota(pack_shape, 0), iota(pack_shape, 1)
    picked = (
        (jnp.broadcast_to(named, pack_shape) == (pack_row // 8).astype(F32))
        & (jnp.broadcast_to(order, pack_shape) == (pack_row % 2).astype(F32))
        & (pack_row // 2 % 2 == pack_col // 64) & (pack_row // 4 % 2 == pack_col % 2)
    )
    packed = jnp.dot(one_hot(picked), gated, preferred_element_type=F32).reshape(planes, 8, lanes)
    blocks = scales.shape[1]
    high = scales[...].astype(BF16).astype(F32)
    scale_rows[...] = jnp.zeros(scale_rows.shape, F32)
    scale_rows[0:1, :blocks] = high
    scale_rows[1:2, :blocks] = scales[...] - high
    disp[...] = jnp.concatenate(
        [packed, jnp.broadcast_to(scale_rows[...][None], (planes, 8, lanes))], axis=1
    ).astype(BF16)
    wide_weights[...] = jnp.zeros(wide_weights.shape, BF16)
    pl.semaphore_wait(
        pltpu.get_barrier_semaphore(),
        (planes - 1) + (count - 1) + per - (z // per == t).astype(jnp.int32),
    )

    for i in range(1, 4):
        quad_copy(i).start()
    loop(1, 2 * groups, lambda j: w_copy(j).start())
    code_copy().start()
    quad[home] = quarters[home]
    for i in range(1, 4):
        quad_copy(i).wait()
    for i in range(4):
        ring[z, i * 32:(i + 1) * 32, :] = quad[i, :32, :]
    ring[z, 128:, :] = quad[0, 32:, :] + quad[1, 32:, :] + quad[2, 32:, :] + quad[3, 32:, :]
    for d in range(1, STRIDE + 1):
        right_seed(d).start()
        left_seed(d).start()
    loop(1, planes, lambda d: disp_copy(d).start())
    slots[z] = disp[z]

    def code_group(index):
        g = (z // per + ((index + 1) // 2) * (2 * (index % 2) - 1) + groups) % groups
        block = ring[pl.ds(g * per, per)]
        rows = per * 64
        tag_block = block[:, 128:, :].reshape(per * 16, lanes)
        lane_in, lane_out = iota((lanes, 4 * lanes), 0), iota((lanes, 4 * lanes), 1)
        names = []
        for h in range(4):
            pick = one_hot(lane_in == h * 32 + (lane_out // lanes) * 8)
            spread = jnp.dot(tag_block, pick, preferred_element_type=F32)
            names.append(spread.reshape(per, 1, 16, 4 * lanes))
        names = jnp.concatenate(names, axis=1).reshape(rows, 4 * lanes)
        upper = jnp.where(iota((rows, 4 * lanes), 1) % lanes >= 64, 1.0, 0.0)
        names = (names - upper).astype(BF16)
        lane_in, lane_out = iota((lanes, 2 * lanes), 0), iota((lanes, 2 * lanes), 1)
        double = one_hot(lane_in == (lane_out // lanes) * 64 + lane_out % 64)
        parts = block[:, :128, :].reshape(per, 4, 2, 16, lanes)
        values, tagged = [], []
        for m in range(2):
            both = jnp.dot(
                parts[:, :, m].reshape(rows, lanes), double, preferred_element_type=F32
            ).astype(BF16)
            for j in range(2):
                values.append(both[:, j * lanes:(j + 1) * lanes])
                tagged.append(names[:, (m * 2 + j) * lanes:(m * 2 + j + 1) * lanes])
        for pair in range(planes // 2):
            chosen = jnp.zeros((rows, lanes), BF16)
            for value, name in zip(values, tagged):
                chosen = jnp.where(name == jnp.asarray(2.0 * pair, BF16), value, chosen)
            wide[:, pair * lanes:(pair + 1) * lanes] = chosen
        result = jnp.dot(wide[...], wide_weights[...], preferred_element_type=F32)
        cols = wide_weights.shape[1]
        result = result.reshape(per, 4, 2, 8, cols).sum(axis=2)
        for h in range(4):
            code_out[g, h] = result[:, h].reshape(per * 8, cols).astype(BF16)
        for h in range(4):
            to = ((h // 2) * groups + g) * 2 + h % 2
            leaves = to != me

            @pl.when(leaves)
            def _():
                plane_copy((to - me + count) % count).start()

            @pl.when(jnp.logical_not(leaves))
            def _():
                gathered[me] = code_out[g, h]

    ring_steps(1, 9)
    loop(1, planes, lambda d: disp_copy(d).wait())
    acts[t] = slots[...].astype(F32)[:, :8, :].reshape(planes * 8, lanes).astype(BF16)
    loop(1, groups, lambda j: tp_copy(j).start())
    ring_steps(9, 10)

    own_codes.wait()
    code_copy().wait()
    spot_in, spot_out = iota((lanes, 2 * lanes), 0), iota((lanes, 2 * lanes), 1)
    column = (2 * z + spot_out // lanes) * narrow + spot_out % lanes
    spot = one_hot((column // lanes == spot_in) & (spot_out % lanes < narrow))
    spread = jnp.dot(
        slots[...].reshape(planes * 16, lanes), spot, preferred_element_type=F32
    ).reshape(planes, 16, 2 * lanes)
    column_scales[...] = spread[:, 8:9, :] + spread[:, 9:10, :]

    def scale_expert(e):
        at = pl.ds(pl.multiple_of(e * 64, 64), 64)
        for x in range(2):
            scale = column_scales[e, :, x * lanes:x * lanes + narrow]
            wide_weights[at, x * lanes:x * lanes + narrow] = (
                swapped[x, e].astype(F32) * scale
            ).astype(BF16)

    loop(0, planes, scale_expert)
    ring_steps(10, 11)
    loop(0, 1, code_group)
    ring_steps(11, 12)
    own_w.wait()
    pair_copy(0).start()

    def pass_on(j):
        w_copy(j).wait_recv()
        pair_copy(j).start()

    loop(1, 2 * groups, pass_on)
    ring_steps(12, 13)
    ring_steps(13, left_last - STRIDE + 1)
    for o in range(left_last - STRIDE + 1, right_last - STRIDE + 1):
        right_wait(o)
        right_next(o).start()

    loop(1, groups, lambda j: tp_copy(j).wait())
    loop(0, 2 * groups, lambda j: pair_copy(j).wait())
    left = jnp.concatenate([acts[g] for g in range(groups)], axis=1)
    first = iota((planes, 8, lanes), 1) < 4
    lines = []
    for c in range(0, width, 2 * lanes):
        wide_cols = min(2 * lanes, width - c)
        zero, one = [
            jnp.dot(
                left,
                weights[p * groups:(p + 1) * groups, :, c:c + wide_cols].reshape(groups * lanes, wide_cols),
                preferred_element_type=F32,
            ).reshape(planes, 8, wide_cols)
            for p in range(2)
        ]
        blank = jnp.zeros((planes, 8, lanes), F32)
        zero_next, one_next = (zero[:, :, lanes:], one[:, :, lanes:]) if wide_cols > lanes else (blank, blank)
        stay = jnp.where(first, zero[:, :, :lanes], one_next)
        move = jnp.where(first, zero_next, one[:, :, :lanes])
        lines.append(stay + pltpu.roll(move, 4, 1))
    base_out[...] = jnp.concatenate(lines, axis=1).astype(BF16)
    loop(1, planes, lambda d: base_copy(d).start())
    base_in[z] = base_out[z]

    loop(1, 5, code_group)
    for o in range(right_last - STRIDE + 1, right_last + 1):
        right_wait(o)
    for o in range(left_last - STRIDE + 1, left_last + 1):
        left_wait(o)
    loop(5, groups, code_group)

    loop(1, count, lambda j: plane_copy(j).wait())

    def add(j, running):
        return running + gathered[j].astype(F32)

    total[...] = lax.fori_loop(0, count, add, jnp.zeros(total.shape, F32))
    for i in range(per):
        @pl.when(jnp.logical_not(stays(i)))
        def _():
            home_copy(i).start()

        @pl.when(stays(i))
        def _():
            code_in[i] = total[i * 8:(i + 1) * 8, :]

    loop(1, 2 * groups, lambda j: w_copy(j).wait_send())
    for d in range(1, STRIDE + 1):
        right_seed(d).wait_send()
        left_seed(d).wait_send()
    loop(1, right_last - STRIDE + 1, lambda o: right_next(o).wait_send())
    loop(1, left_last - STRIDE + 1, lambda o: left_next(o).wait_send())
    loop(1, planes, lambda d: base_copy(d).wait())
    for i in range(per):
        @pl.when(jnp.logical_not(stays(i)))
        def _():
            home_copy(i).wait_send()
            home_arrival(i).wait_recv()


def shards(base_weight, delta_codes, block_scales, hidden_acts, expert_ids, gate_weights):
    groups = lax.axis_size("tp")
    planes = lax.axis_size("fsdp") // 2
    steps, rows, top = expert_ids.shape
    units = hidden_acts.shape[4]
    width = base_weight.shape[2]
    narrow = delta_codes.shape[2]
    block_count = block_scales.shape[2]
    capacity = 2
    slot_count = rows * top
    per = planes // groups
    total_slots = steps * slot_count

    dma = pltpu.SemaphoreType.DMA
    vmem = pl.BlockSpec(memory_space=pltpu.VMEM)
    outside = pl.BlockSpec(memory_space=pltpu.HBM)
    count = 4 * groups

    def body(*refs):
        resync_kernel(planes, groups, *refs)

    base_in, code_in = pl.pallas_call(
        body,
        out_shape=(
            jax.ShapeDtypeStruct((planes, 32, 128), BF16),
            jax.ShapeDtypeStruct((per, 8, 256), F32),
        ),
        in_specs=[vmem, vmem, vmem, vmem, outside, outside],
        out_specs=(vmem, vmem),
        scratch_shapes=[
            pltpu.VMEM((8, 128), F32),
            pltpu.VMEM((planes, 16, 128), BF16),
            pltpu.VMEM((4, 48, 128), BF16),
            pltpu.VMEM((4, 48, 128), BF16),
            pltpu.VMEM((planes, 16, 128), BF16),
            pltpu.VMEM((planes, 144, 128), BF16),
            pltpu.VMEM((2 * groups, units, width // groups), BF16),
            pltpu.VMEM((2, planes, 64, narrow), BF16),
            pltpu.VMEM((planes, 1, 256), F32),
            pltpu.VMEM((planes * 64, 256), BF16),
            pltpu.VMEM((per * 64, planes * 64), BF16),
            pltpu.VMEM((groups, planes * 8, units), BF16),
            pltpu.VMEM((planes, 32, 128), BF16),
            pltpu.VMEM((groups, 4, per * 8, 256), BF16),
            pltpu.VMEM((count, per * 8, 256), BF16),
            pltpu.VMEM((per * 8, 256), F32),
            dma((2,)),
            dma((4,)), dma((4,)),
            dma((planes,)), dma((planes,)),
            dma((groups,)), dma((groups,)),
            dma((2 * groups,)), dma((2 * groups,)),
            dma((2 * groups,)), dma((2 * groups,)),
            dma, dma,
            dma((planes,)), dma((planes,)), dma((planes,)), dma((planes,)),
            dma((planes,)), dma((planes,)),
            dma((count,)), dma((count,)),
            dma((per,)), dma((per,)),
        ],
        compiler_params=pltpu.CompilerParams(
            collective_id=0, has_side_effects=True, vmem_limit_bytes=62 << 20
        ),
    )(
        hidden_acts.reshape(total_slots * 2, units),
        expert_ids.reshape(steps * rows, top),
        gate_weights.reshape(steps * rows, top),
        block_scales.reshape(1, block_count),
        base_weight.reshape(units, width),
        delta_codes.reshape(planes, 2, 64, narrow),
    )

    flat_ids = expert_ids.reshape(steps, slot_count)
    slot_index = jnp.arange(slot_count, dtype=jnp.int32)
    earlier = (flat_ids[:, :, None] == flat_ids[:, None, :]) & (
        slot_index[None, None, :] < slot_index[None, :, None]
    )
    order = jnp.sum(earlier.astype(jnp.int32), axis=2)
    select = (
        flat_ids[:, None, None, :] == jnp.arange(planes, dtype=jnp.int32)[None, :, None, None]
    ) & (order[:, None, None, :] == jnp.arange(capacity, dtype=jnp.int32)[None, None, :, None])
    row_select = select.reshape(steps, planes, capacity, rows, top).astype(F32).sum(axis=4).astype(BF16)
    blocks = width // groups // 128
    back = base_in[:, :4 * blocks].reshape(planes, blocks, steps, capacity, 128)
    mixed = jnp.einsum("secn,ebscl->snbl", row_select, back, preferred_element_type=F32)
    coded = (
        code_in.reshape(per, steps, rows, 2, 128)[..., :narrow]
        .transpose(1, 2, 0, 3, 4)
        .reshape(steps, rows, width // groups)
    )
    return (mixed.reshape(steps, rows, width // groups) + coded).astype(BF16)


def solution(mesh):
    placed = (
        P("fsdp", "tp", None),
        P(None, ("tp", "rep"), "fsdp"),
        P("fsdp", "tp", None),
        P(None, ("fsdp", "rep"), None, None, "tp"),
        P(None, ("fsdp", "rep"), None),
        P(None, ("fsdp", "rep"), None),
    )
    return jax.shard_map(
        shards,
        mesh=mesh,
        in_specs=placed,
        out_specs=P(None, ("fsdp", "rep"), "tp"),
        check_vma=False,
    )
```
